256 devices in a mesh: dp: 16 (over z, core), node: 16 (over y, x).
Axes of the slice: x: 4, y: 4, z: 8, core: 2. Of those that a mesh axis runs over, the one named last changes fastest.
Arguments:
- node_state: bfloat16 [131072, 1024], P(('dp', 'node')), parts along dimension 0, may hold values from -6 to 6
- edge_recv: int32 [1048576], P(('dp', 'node')), parts along dimension 0, may hold values from 0 to 511
- edge_send: int32 [1048576], P(('dp', 'node')), parts along dimension 0, may hold values from 0 to 2559
- halo_rows: int32 [256, 16, 128], P(('dp', 'node')), parts along dimension 0, may hold values from 0 to 511
- window_reach: int32 [16], replicated, may hold values from 32 to 128
- w_recv: bfloat16 [1024, 512], replicated, may hold values from -0.1875 to 0.1875
- w_send: bfloat16 [1024, 512], replicated, may hold values from -0.1875 to 0.1875
- edge_bias: float32 [512], replicated, may hold values from -4 to 4
- w_message: bfloat16 [512, 512], replicated, may hold values from -0.25 to 0.25
- msg_gain: float32 [512], replicated, may hold values from 0.5 to 2
- w_lift: bfloat16 [512, 1024], replicated, may hold values from -0.25 to 0.25
- attn_gain: float32 [1024], replicated, may hold values from 0.5 to 2
- w_qkv: bfloat16 [1024, 16, 192], replicated, may hold values from -1 to 1
- w_out: bfloat16 [1024, 1024], replicated, may hold values from -0.1875 to 0.1875
Outputs:
- result: bfloat16 [131072, 1024], P(('dp', 'node')), parts along dimension 0
The draws below stay inside these ranges and needn't reach their ends.
There are 16 independent parts, one for each index of `dp`. The reference program is written for one: setup_inputs(seed, part) draws one part's arguments, and reference() takes and returns one part's arrays. A program takes and returns all parts, laid end to end along the dimension named above; an argument that names none is the same for every part. Nothing has to cross between parts.
All inputs are finite; a program needn't handle non-finite values.
Results may differ from the reference program's by a relative error of at most 0.0085.
Values may be sent and summed in bfloat16 or wider, within the bound.
No kernel may reach another device: no remote copies, remote signals or barrier semaphores. Data moves between devices by JAX's collectives and lax.ppermute only.
A program may use at most 128 MiB of HBM per device.

```python
import math
import jax
import jax.numpy as jnp
from jax import lax

D = 1024
M = 512
HEADS = 16
HD = 64
NODE_DEV = 512
WIN_MAX = 128
HALO = 128
NODE_GROUP = 16
N = 8192
E_ALL = 65536
SLOTS = 2560
N_NODE = 16


def draw_edge_send(key, part):
    key = jax.random.fold_in(key, 7)
    first, second, third = jax.random.split(key, 3)
    local = jax.random.randint(first, (E_ALL,), 0, NODE_DEV)
    remote = NODE_DEV + jax.random.randint(second, (E_ALL,), 0, NODE_GROUP * HALO)
    pick = jax.random.randint(third, (E_ALL,), 0, 5) < 2
    chosen = jnp.where(pick, remote, local)
    chosen = chosen.at[0].set(SLOTS - 1).at[1].set(0)
    return chosen.astype(jnp.int32)


def draw_window_reach(key, part):
    key = jax.random.fold_in(key, 5)
    first, second = jax.random.split(key)
    reach = jax.random.randint(first, (HEADS,), WIN_MAX // 4, WIN_MAX + 1)
    spot = jax.random.randint(second, (), 0, HEADS)
    return jnp.where(jnp.arange(HEADS) == spot, WIN_MAX, reach).astype(jnp.int32)


def draw_w_qkv(key, part):
    key = jax.random.fold_in(key, 11)
    first, second, third = jax.random.split(key, 3)
    factor = D ** (-0.5)
    query = factor * jax.random.normal(first, (D, HEADS, HD), jnp.float32)
    keys = factor * jax.random.normal(second, (D, HEADS, HD), jnp.float32)
    values = factor * jax.random.normal(third, (D, HEADS, HD), jnp.float32)
    whole = jnp.concatenate([query, keys, values], axis=2)
    return jnp.clip(whole, -1.0, 1.0).astype(jnp.bfloat16)


def touch_ends(entries, key, low, high):
    shape = entries.shape
    spot = [jax.random.randint(jax.random.fold_in(key, axis), (), 0, shape[axis]) for axis in range(len(shape))]
    entries = entries.at[tuple(spot)].set(low)
    longest = shape.index(max(shape))
    spot[longest] = (spot[longest] + 1) % shape[longest]
    return entries.at[tuple(spot)].set(high)


def levels(own_key, extent, pieces, least, top_value):
    factor_of = 1.0
    for axis_at, parts in pieces:
        heights = jax.random.uniform(jax.random.fold_in(jax.random.fold_in(own_key, 6), axis_at), (parts,), jnp.float32, least / len(pieces), top_value / len(pieces))
        factor_of = factor_of * jnp.repeat(jnp.exp(heights), extent[axis_at] // parts).reshape((-1,) + (1,) * (len(extent) - 1 - axis_at))
    return factor_of


def noise(rng, shape, deviation, bound, shards=(), held_as=jnp.bfloat16):
    level = levels(rng, shape, shards, -0.22, 0.18) if shards else 1.0
    array = jax.random.normal(rng, shape, jnp.float32) * deviation * level
    return jnp.minimum(jnp.maximum(array, -bound), bound).astype(held_as)


def setup_inputs(seed: int = 0, part: int = 0) -> dict:
    key_of = jax.random.split(jax.random.key(seed), 15)
    part_keys = jax.random.split(jax.random.fold_in(key_of[14], part), 15)
    node_state = noise(part_keys[0], (N, D), 1.0, 6.0, ((0, 16),))
    edge_recv = touch_ends(jax.random.randint(part_keys[1], (E_ALL,), 0, NODE_DEV), jax.random.fold_in(part_keys[1], 1), 0, NODE_DEV - 1).astype(jnp.int32)
    edge_send = draw_edge_send(jax.random.fold_in(jax.random.fold_in(key_of[14], part), 71), part)
    halo_rows = touch_ends(jax.random.randint(part_keys[3], (NODE_GROUP, NODE_GROUP, HALO), 0, NODE_DEV), jax.random.fold_in(part_keys[3], 1), 0, NODE_DEV - 1).astype(jnp.int32)
    window_reach = draw_window_reach(jax.random.fold_in(key_of[14], 71), part)
    w_recv = noise(key_of[5], (D, M), D ** -0.5, 0.1875)
    w_send = noise(key_of[6], (D, M), D ** -0.5, 0.1875)
    edge_bias = noise(key_of[7], (M,), 0.7, 4.0, (), jnp.float32)
    w_message = noise(key_of[8], (M, M), M ** -0.5, 0.25)
    msg_gain = jnp.clip(jnp.exp(jax.random.uniform(key_of[9], (M,), jnp.float32, math.log(0.5), math.log(2.0))), 0.5, 2.0)
    w_lift = noise(key_of[10], (M, D), M ** -0.5, 0.25)
    attn_gain = jnp.clip(jnp.exp(jax.random.uniform(key_of[11], (D,), jnp.float32, math.log(0.5), math.log(2.0))), 0.5, 2.0)
    w_qkv = draw_w_qkv(jax.random.fold_in(key_of[14], 71), part)
    w_out = noise(key_of[13], (D, D), D ** -0.5, 0.1875)
    return {"node_state": node_state, "edge_recv": edge_recv, "edge_send": edge_send, "halo_rows": halo_rows, "window_reach": window_reach, "w_recv": w_recv, "w_send": w_send, "edge_bias": edge_bias, "w_message": w_message, "msg_gain": msg_gain, "w_lift": w_lift, "attn_gain": attn_gain, "w_qkv": w_qkv, "w_out": w_out}


def rms_scale(values, gain):
    mean_sq = lax.optimization_barrier(jnp.mean(values * values, axis=-1, keepdims=True))
    return values * lax.rsqrt(mean_sq + 1e-05) * gain

def attend(query, keys, values, reach, q_start, k_start, total):
    q_pos = q_start + jnp.arange(query.shape[0], dtype=jnp.int32)
    k_pos = k_start + jnp.arange(keys.shape[0], dtype=jnp.int32)
    apart = jnp.abs(q_pos[:, None] - k_pos[None, :])
    inside = (k_pos >= 0) & (k_pos < total)
    valid = (apart[None, :, :] <= reach[:, None, None]) & inside[None, None, :]
    score = jnp.einsum('qhd,khd->hqk', query.astype(jnp.float32), keys.astype(jnp.float32)) * query.shape[2] ** (-0.5)
    score = jnp.where(valid, score, -1e+30)
    top = lax.optimization_barrier(jnp.max(score, axis=-1, keepdims=True))
    expo = jnp.where(valid, jnp.exp(score - top), 0.0)
    weights = (expo / lax.optimization_barrier(jnp.sum(expo, axis=-1, keepdims=True))).astype(jnp.bfloat16)
    mixed = jnp.einsum('hqk,khd->qhd', weights.astype(jnp.float32), values.astype(jnp.float32))
    return mixed.astype(jnp.bfloat16)

def reference(node_state, edge_recv, edge_send, halo_rows, window_reach, w_recv, w_send, edge_bias, w_message, msg_gain, w_lift, attn_gain, w_qkv, w_out):
    total = node_state.shape[0]
    rows = total // N_NODE
    halo = halo_rows.shape[2]
    recv_proj = jnp.dot(node_state, w_recv, preferred_element_type=jnp.float32).astype(jnp.bfloat16)
    send_proj = jnp.dot(node_state, w_send, preferred_element_type=jnp.float32).astype(jnp.bfloat16)
    owner = (jnp.arange(edge_recv.shape[0], dtype=jnp.int32) // (edge_recv.shape[0] // N_NODE)).astype(jnp.int32)
    receivers = owner * rows + edge_recv
    slot = jnp.maximum(edge_send - rows, 0)
    peer = slot // halo
    place = slot % halo
    remote = peer * rows + halo_rows[peer, owner, place]
    senders = jnp.where(edge_send < rows, owner * rows + edge_send, remote).astype(jnp.int32)
    pre = recv_proj[receivers].astype(jnp.float32) + send_proj[senders].astype(jnp.float32) + edge_bias
    message = jax.nn.silu(pre).astype(jnp.bfloat16)
    mixed = jnp.dot(message, w_message, preferred_element_type=jnp.float32).astype(jnp.bfloat16)
    aggregate = jax.ops.segment_sum(mixed.astype(jnp.float32), receivers, num_segments=total)
    normed = rms_scale(aggregate, msg_gain).astype(jnp.bfloat16)
    state = (node_state.astype(jnp.float32) + jnp.dot(normed, w_lift, preferred_element_type=jnp.float32)).astype(jnp.bfloat16)
    attn_in = rms_scale(state.astype(jnp.float32), attn_gain).astype(jnp.bfloat16)
    qkv = jnp.einsum('rd,dhc->rhc', attn_in.astype(jnp.float32), w_qkv.astype(jnp.float32)).astype(jnp.bfloat16)
    width = qkv.shape[2] // 3
    query = qkv[:, :, :width]
    padded = jnp.pad(qkv[:, :, width:], ((WIN_MAX, WIN_MAX), (0, 0), (0, 0)))
    block = min(512, total)

    def one_block(index):
        start = (index * block).astype(jnp.int32)
        q_part = lax.dynamic_slice_in_dim(query, start, block, 0)
        kv_part = lax.dynamic_slice_in_dim(padded, start, block + 2 * WIN_MAX, 0)
        return attend(q_part, kv_part[:, :, :width], kv_part[:, :, width:], window_reach, start, start - WIN_MAX, total)
    attended = lax.map(one_block, jnp.arange(total // block, dtype=jnp.int32))
    attended = attended.reshape(total, -1)
    result = state.astype(jnp.float32) + jnp.dot(attended, w_out, preferred_element_type=jnp.float32)
    return result.astype(jnp.bfloat16)
```

```python
import functools

import jax
import jax.numpy as jnp
from jax import lax
from jax.experimental import pallas as pl
from jax.experimental.pallas import tpu as pltpu
from jax.sharding import PartitionSpec as P

WIN = 128
TILE = 256
CHUNK = 256
BIG = 1 << 20
NEG = -1e30
F32 = jnp.float32
BF16 = jnp.bfloat16
VMEM = pl.BlockSpec(memory_space=pltpu.VMEM)
SMEM = pl.BlockSpec(memory_space=pltpu.SMEM)
ANY = pl.BlockSpec(memory_space=pl.ANY)
LIMIT = 44 * 1024 * 1024


def dot(a, b):
    return jnp.dot(a, b, preferred_element_type=F32)


def dot_nt(a, b):
    return lax.dot_general(a, b, (((1,), (1,)), ((), ())), preferred_element_type=F32)


def onehot(index, size):
    place = lax.broadcasted_iota(jnp.int32, (size, index.shape[1]), 0)
    return jnp.where(place == index, 1.0, 0.0).astype(BF16)


def rms_scale(values, gain):
    mean_sq = jnp.mean(values * values, axis=-1, keepdims=True)
    return values * lax.rsqrt(mean_sq + 1e-05) * gain


def send_kernel(x_ref, w_ref, halo_ref, table_ref, out_ref):
    proj = dot(x_ref[...], w_ref[...])
    proj_t = jnp.transpose(proj).astype(BF16)
    for part in range(table_ref.shape[0]):
        table_ref[part] = proj_t[:, part * 128 : (part + 1) * 128]
    rows = x_ref.shape[0]
    for pair in range(out_ref.shape[0] // 2):
        hot = jnp.concatenate(
            [onehot(halo_ref[pl.ds(2 * pair + k, 1), :], rows) for k in range(2)], axis=1
        )
        picked = dot(proj_t, hot).astype(BF16)
        out_ref[2 * pair] = picked[:, :128]
        out_ref[2 * pair + 1] = picked[:, 128:]


def edge_tiles(first, last, ends_ref, keys_ref, table_ref, recv_ref, bias_ref, pre_ref, agg_ref):
    rows = recv_ref.shape[1]

    def chunk_of(index, slot):
        chunk = jnp.concatenate([table_ref[2 * index], table_ref[2 * index + 1]], axis=1)
        return dot(chunk, onehot(slot - index * CHUNK, CHUNK))

    def body(tile, carry):
        key = keys_ref[tile]
        recv = (key >> 8) & 511
        slot = ((key >> 17) << 8) | (key & 255)
        low = ends_ref[2 * tile]
        high = ends_ref[2 * tile + 1]
        hot = onehot(recv, rows)
        bias = bias_ref[...]
        pre_ref[...] = (
            dot(recv_ref[...], hot)
            + chunk_of(low, slot)
            + jnp.concatenate([bias] * (TILE // 128), axis=1)
        )

        def more(index, inner):
            pre_ref[...] += chunk_of(index, slot)
            return inner

        lax.fori_loop(low + 1, high + 1, more, 0)
        half = 0.5 * pre_ref[...]
        message = (half + half * jnp.tanh(half)).astype(BF16)
        agg_ref[...] += dot_nt(hot, message)
        return carry

    lax.fori_loop(first, last, body, 0)


def local_tiles(ends_ref, tiles, local_chunks):
    def count(tile, total):
        return total + jnp.where(ends_ref[2 * tile + 1] < local_chunks, 1, 0)

    return lax.fori_loop(0, tiles, count, 0)


def local_kernel(
    ends_ref, keys_ref, x_ref, w_ref, bias_ref, table_ref, recv_ref, agg_ref, pre_ref, bias_wide
):
    proj = dot(x_ref[...], w_ref[...])
    recv_ref[...] = jnp.transpose(proj).astype(BF16)
    bias_wide[...] = jnp.broadcast_to(bias_ref[...], bias_wide.shape)
    agg_ref[...] = jnp.zeros_like(agg_ref)
    tiles = keys_ref.shape[0]
    split = local_tiles(ends_ref, tiles, x_ref.shape[0] // CHUNK)
    edge_tiles(0, split, ends_ref, keys_ref, table_ref, recv_ref, bias_wide, pre_ref, agg_ref)


def finish_rows(agg, x, w_message, msg_gain, w_lift, attn_gain):
    high = agg.astype(BF16)
    low = (agg - high.astype(F32)).astype(BF16)
    mixed = dot(high, w_message) + dot(low, w_message)
    normed = rms_scale(mixed, msg_gain).astype(BF16)
    state = (x.astype(F32) + dot(normed, w_lift)).astype(BF16)
    return state, rms_scale(state.astype(F32), attn_gain).astype(BF16)


def remote_kernel(
    ends_ref,
    keys_ref,
    x_ref,
    bias_ref,
    recv_ref,
    agg_in_ref,
    msg_gain_ref,
    attn_gain_ref,
    sent_hbm,
    come_hbm,
    w_message_hbm,
    w_lift_hbm,
    agg_mid_ref,
    state_ref,
    top_ref,
    bottom_ref,
    table_ref,
    w_message,
    w_lift,
    agg_ref,
    pre_ref,
    bias_wide,
    sems,
):
    own = sent_hbm.shape[0]
    copies = [
        pltpu.make_async_copy(sent_hbm, table_ref.at[pl.ds(0, own)], sems.at[0]),
        pltpu.make_async_copy(come_hbm, table_ref.at[pl.ds(own, come_hbm.shape[0])], sems.at[1]),
        pltpu.make_async_copy(w_message_hbm, w_message, sems.at[2]),
        pltpu.make_async_copy(w_lift_hbm, w_lift, sems.at[3]),
    ]
    for copy in copies:
        copy.start()
    agg_ref[...] = agg_in_ref[...]
    bias_wide[...] = jnp.broadcast_to(bias_ref[...], bias_wide.shape)
    tiles = keys_ref.shape[0]
    split = local_tiles(ends_ref, tiles, x_ref.shape[0] // CHUNK)
    copies[0].wait()
    copies[1].wait()
    edge_tiles(split, tiles, ends_ref, keys_ref, table_ref, recv_ref, bias_wide, pre_ref, agg_ref)
    copies[2].wait()
    copies[3].wait()
    rows = x_ref.shape[0]
    agg_mid_ref[...] = agg_ref[pl.ds(WIN, rows - 2 * WIN), :]
    agg = jnp.concatenate([agg_ref[:WIN], agg_ref[rows - WIN :]], axis=0)
    x = jnp.concatenate([x_ref[:WIN], x_ref[rows - WIN :]], axis=0)
    state, attn_in = finish_rows(
        agg, x, w_message[...], msg_gain_ref[...], w_lift[...], attn_gain_ref[...]
    )
    state_ref[...] = state
    top_ref[...] = attn_in[:WIN]
    bottom_ref[...] = attn_in[WIN:]


def attend(q, k, v, apart, reach, scale):
    lane = lax.broadcasted_iota(jnp.int32, q.shape, 1)
    zero = jnp.zeros_like(q)
    both = jnp.concatenate([jnp.where(lane < 64, q, zero), jnp.where(lane >= 64, q, zero)], axis=0)
    score = dot_nt(both, k)
    parts = []
    rows = q.shape[0]
    for head in range(2):
        one = score[head * rows : (head + 1) * rows]
        one = jnp.where(apart <= reach[head], one, NEG)
        top = jnp.max(one, axis=-1, keepdims=True)
        parts.append(jnp.exp2((one - top) * scale).astype(BF16))
    weights = jnp.concatenate(parts, axis=0)
    wide = jnp.concatenate([v, jnp.ones((v.shape[0], 128), BF16)], axis=1)
    mixed = dot(weights, wide)
    out = mixed[:, :128] / mixed[:, 128:]
    return jnp.where(lane < 64, out[:rows], out[rows:]).astype(BF16)


def distance(rows, keys):
    q_at = lax.broadcasted_iota(jnp.int32, (rows, keys), 0) + WIN
    k_at = lax.broadcasted_iota(jnp.int32, (rows, keys), 1)
    return jnp.abs(q_at - k_at), k_at


LOG2E = 1.4426950408889634


def inner_kernel(
    reach_ref,
    agg_ref,
    x_ref,
    state_tb_ref,
    top_ref,
    bottom_ref,
    msg_gain_ref,
    attn_gain_ref,
    w_message_hbm,
    w_lift_hbm,
    w_q_hbm,
    w_k_hbm,
    w_v_hbm,
    w_out_hbm,
    q_ref,
    k_ref,
    v_ref,
    res_ref,
    w_message,
    w_lift,
    w_q,
    w_k,
    w_v,
    w_out,
    attn_ref,
    q_mid,
    mix_ref,
    apart_ref,
    sems,
):
    pairs = [
        (w_message_hbm, w_message),
        (w_lift_hbm, w_lift),
        (w_q_hbm, w_q),
        (w_k_hbm, w_k),
        (w_v_hbm, w_v),
        (w_out_hbm, w_out),
    ]
    copies = [pltpu.make_async_copy(a, b, sems.at[i]) for i, (a, b) in enumerate(pairs)]
    for copy in copies:
        copy.start()
    rows = x_ref.shape[0]
    mid = rows - 2 * WIN
    copies[0].wait()
    copies[1].wait()
    state, attn_in = finish_rows(
        agg_ref[...],
        x_ref[pl.ds(WIN, mid), :],
        w_message[...],
        msg_gain_ref[...],
        w_lift[...],
        attn_gain_ref[...],
    )
    attn_ref[pl.ds(0, WIN), :] = top_ref[...]
    attn_ref[pl.ds(rows - WIN, WIN), :] = bottom_ref[...]
    attn_ref[pl.ds(WIN, mid), :] = attn_in
    copies[2].wait()
    q = dot(attn_ref[...], w_q[...]).astype(BF16)
    q_ref[pl.ds(0, WIN), :] = q[:WIN]
    q_ref[pl.ds(WIN, WIN), :] = q[rows - WIN :]
    q_mid[...] = q[WIN : rows - WIN]
    copies[3].wait()
    k_ref[...] = dot(attn_ref[...], w_k[...]).astype(BF16)
    copies[4].wait()
    v_ref[...] = dot(attn_ref[...], w_v[...]).astype(BF16)
    apart_ref[...] = distance(WIN, 3 * WIN)[0]

    def body(pair, carry):
        lanes = pl.ds(pl.multiple_of(pair * 128, 128), 128)
        reach = (reach_ref[2 * pair], reach_ref[2 * pair + 1])
        for block in range(2):
            keys = pl.ds(block * WIN, 3 * WIN)
            mix_ref[pl.ds(block * WIN, WIN), lanes] = attend(
                q_mid[pl.ds(block * WIN, WIN), lanes],
                k_ref[keys, lanes],
                v_ref[keys, lanes],
                apart_ref[...],
                reach,
                0.125 * LOG2E,
            )
        return carry

    lax.fori_loop(0, q_ref.shape[1] // 128, body, 0)
    copies[5].wait()
    res_ref[...] = (state.astype(F32) + dot(mix_ref[...], w_out[...])).astype(BF16)


def outer_kernel(
    reach_ref,
    q_ref,
    left_ref,
    right_ref,
    k_ref,
    v_ref,
    state_ref,
    w_k_hbm,
    w_v_hbm,
    w_out_hbm,
    res_hbm,
    out_hbm,
    w_k,
    w_v,
    w_out,
    keys_ref,
    values_ref,
    apart_ref,
    mix_ref,
    fin_ref,
    sems,
):
    rows = k_ref.shape[0]
    pairs = [
        (w_k_hbm, w_k),
        (w_v_hbm, w_v),
        (w_out_hbm, w_out),
        (res_hbm, out_hbm.at[pl.ds(WIN, rows - 2 * WIN)]),
    ]
    copies = [pltpu.make_async_copy(a, b, sems.at[i]) for i, (a, b) in enumerate(pairs)]
    for copy in copies:
        copy.start()
    halo = jnp.concatenate([left_ref[...], right_ref[...]], axis=0)
    two = 2 * WIN
    keys_ref[0, pl.ds(WIN, two), :] = k_ref[pl.ds(0, two), :]
    keys_ref[1, pl.ds(0, two), :] = k_ref[pl.ds(rows - two, two), :]
    values_ref[0, pl.ds(WIN, two), :] = v_ref[pl.ds(0, two), :]
    values_ref[1, pl.ds(0, two), :] = v_ref[pl.ds(rows - two, two), :]
    apart, k_at = distance(WIN, 3 * WIN)
    heads = reach_ref.shape[0] - 2
    apart_ref[0] = jnp.where((k_at < WIN) & (reach_ref[heads] != 0), BIG, apart)
    apart_ref[1] = jnp.where((k_at >= two) & (reach_ref[heads + 1] != 0), BIG, apart)
    copies[0].wait()
    k_halo = dot(halo, w_k[...]).astype(BF16)
    keys_ref[0, pl.ds(0, WIN), :] = k_halo[:WIN]
    keys_ref[1, pl.ds(two, WIN), :] = k_halo[WIN:]
    copies[1].wait()
    v_halo = dot(halo, w_v[...]).astype(BF16)
    values_ref[0, pl.ds(0, WIN), :] = v_halo[:WIN]
    values_ref[1, pl.ds(two, WIN), :] = v_halo[WIN:]

    def body(pair, carry):
        lanes = pl.ds(pl.multiple_of(pair * 128, 128), 128)
        reach = (reach_ref[2 * pair], reach_ref[2 * pair + 1])
        for block in range(2):
            mix_ref[pl.ds(block * WIN, WIN), lanes] = attend(
                q_ref[pl.ds(block * WIN, WIN), lanes],
                keys_ref[block, :, lanes],
                values_ref[block, :, lanes],
                apart_ref[block],
                reach,
                0.125 * LOG2E,
            )
        return carry

    lax.fori_loop(0, q_ref.shape[1] // 128, body, 0)
    copies[2].wait()
    fin_ref[...] = (state_ref[...].astype(F32) + dot(mix_ref[...], w_out[...])).astype(BF16)
    ends = [
        pltpu.make_async_copy(fin_ref.at[pl.ds(0, WIN)], out_hbm.at[pl.ds(0, WIN)], sems.at[4]),
        pltpu.make_async_copy(
            fin_ref.at[pl.ds(WIN, WIN)], out_hbm.at[pl.ds(rows - WIN, WIN)], sems.at[5]
        ),
    ]
    for copy in ends:
        copy.start()
    copies[3].wait()
    for copy in ends:
        copy.wait()


def call(kernel, name, out_shape, in_specs, out_specs, scratch, flops, moved):
    return pl.pallas_call(
        kernel,
        name=name,
        out_shape=out_shape,
        in_specs=in_specs,
        out_specs=out_specs,
        scratch_shapes=scratch,
        compiler_params=pltpu.CompilerParams(vmem_limit_bytes=LIMIT),
        cost_estimate=pl.CostEstimate(flops=flops, bytes_accessed=moved, transcendentals=0),
    )


def local(
    node_state,
    edge_recv,
    edge_send,
    halo_rows,
    window_reach,
    w_recv,
    w_send,
    edge_bias,
    w_message,
    msg_gain,
    w_lift,
    attn_gain,
    w_qkv,
    w_out,
):
    shape = jax.ShapeDtypeStruct
    rows, width = node_state.shape
    hidden = w_recv.shape[1]
    peers, halo = halo_rows.shape[1:]
    edges = edge_recv.shape[0]
    heads = w_qkv.shape[1]
    size = w_qkv.shape[2] // 3
    tiles = edges // TILE
    dma = pltpu.SemaphoreType.DMA
    mega = 1 << 20

    table, outgoing = call(
        send_kernel,
        "send",
        (shape((rows // 128, hidden, 128), BF16), shape((peers, hidden, halo), BF16)),
        [VMEM] * 3,
        (VMEM, VMEM),
        [],
        4 << 30,
        4 * mega,
    )(node_state, w_send, halo_rows.reshape(peers, halo))
    incoming = lax.all_to_all(outgoing, "node", split_axis=0, concat_axis=0, tiled=True)

    keys = lax.sort(((edge_send >> 8) << 17) | (edge_recv << 8) | (edge_send & 255))
    tiled = keys.reshape(tiles, TILE)
    ends = (jnp.stack([tiled[:, 0], tiled[:, -1]], axis=1) >> 17).reshape(-1)
    keys = keys.reshape(tiles, 1, TILE)
    bias = edge_bias.reshape(hidden, 1)
    recv, agg = call(
        local_kernel,
        "local_edges",
        (shape((hidden, rows), BF16), shape((rows, hidden), F32)),
        [SMEM] + [VMEM] * 5,
        (VMEM, VMEM),
        [pltpu.VMEM((hidden, TILE), F32), pltpu.VMEM((hidden, 128), F32)],
        10 << 30,
        4 * mega,
    )(ends, keys, node_state, w_recv, bias, table)
    split_qkv = w_qkv.reshape(width, heads, 3, size)
    w_q, w_k, w_v = (split_qkv[:, :, i].reshape(width, heads * size) for i in range(3))

    gain_m = msg_gain.reshape(1, hidden)
    gain_a = attn_gain.reshape(1, width)
    agg_mid, state_tb, top, bottom = call(
        remote_kernel,
        "remote_edges",
        (
            shape((rows - 2 * WIN, hidden), F32),
            shape((2 * WIN, width), BF16),
            shape((WIN, width), BF16),
            shape((WIN, width), BF16),
        ),
        [SMEM] + [VMEM] * 7 + [ANY] * 4,
        (VMEM,) * 4,
        [
            pltpu.VMEM((rows // 128 + peers, hidden, 128), BF16),
            pltpu.VMEM((hidden, hidden), BF16),
            pltpu.VMEM((hidden, width), BF16),
            pltpu.VMEM((rows, hidden), F32),
            pltpu.VMEM((hidden, TILE), F32),
            pltpu.VMEM((hidden, 128), F32),
            dma((4,)),
        ],
        10 << 30,
        4 * mega,
    )(ends, keys, node_state, bias, recv, agg, gain_m, gain_a, table, incoming, w_message, w_lift)

    nodes = lax.axis_size("node")
    me = lax.axis_index("node")
    left = lax.ppermute(bottom, "node", [(i, (i + 1) % nodes) for i in range(nodes)])
    right = lax.ppermute(top, "node", [(i, (i - 1) % nodes) for i in range(nodes)])
    reach = jnp.concatenate(
        [window_reach, jnp.stack([me == 0, me == nodes - 1]).astype(jnp.int32)]
    )

    q_tb, k, v, res_mid = call(
        inner_kernel,
        "inner",
        (
            shape((2 * WIN, width), BF16),
            shape((rows, width), BF16),
            shape((rows, width), BF16),
            shape((rows - 2 * WIN, width), BF16),
        ),
        [SMEM] + [VMEM] * 7 + [ANY] * 6,
        (VMEM,) * 4,
        [
            pltpu.VMEM((hidden, hidden), BF16),
            pltpu.VMEM((hidden, width), BF16),
            pltpu.VMEM((width, width), BF16),
            pltpu.VMEM((width, width), BF16),
            pltpu.VMEM((width, width), BF16),
            pltpu.VMEM((width, width), BF16),
            pltpu.VMEM((rows, width), BF16),
            pltpu.VMEM((rows - 2 * WIN, width), BF16),
            pltpu.VMEM((rows - 2 * WIN, width), BF16),
            pltpu.VMEM((WIN, 3 * WIN), jnp.int32),
            dma((6,)),
        ],
        10 << 30,
        12 * mega,
    )(
        reach,
        agg_mid,
        node_state,
        state_tb,
        top,
        bottom,
        gain_m,
        gain_a,
        w_message,
        w_lift,
        w_q,
        w_k,
        w_v,
        w_out,
    )

    return call(
        outer_kernel,
        "outer",
        shape((rows, width), BF16),
        [SMEM] + [VMEM] * 6 + [ANY] * 4,
        ANY,
        [
            pltpu.VMEM((width, width), BF16),
            pltpu.VMEM((width, width), BF16),
            pltpu.VMEM((width, width), BF16),
            pltpu.VMEM((2, 3 * WIN, width), BF16),
            pltpu.VMEM((2, 3 * WIN, width), BF16),
            pltpu.VMEM((2, WIN, 3 * WIN), jnp.int32),
            pltpu.VMEM((2 * WIN, width), BF16),
            pltpu.VMEM((2 * WIN, width), BF16),
            dma((6,)),
        ],
        6 << 30,
        12 * mega,
    )(reach, q_tb, left, right, k, v, state_tb, w_k, w_v, w_out, res_mid)


def solution(mesh):
    split = ("dp", "node")
    in_specs = (P(split, None), P(split), P(split), P(split, None, None)) + (P(),) * 10
    return jax.shard_map(
        local, mesh=mesh, in_specs=in_specs, out_specs=P(split, None), check_vma=False
    )
```

```python
import jax
import jax.numpy as jnp
from jax import lax
from jax.experimental import pallas as pl
from jax.experimental.pallas import tpu as pltpu
from jax.sharding import PartitionSpec as P

WIN = 128
TILE = 256
CHUNK = 256
BIG = 1 << 20
NEG = -1e30
F32 = jnp.float32
BF16 = jnp.bfloat16
VMEM = pl.BlockSpec(memory_space=pltpu.VMEM)
SMEM = pl.BlockSpec(memory_space=pltpu.SMEM)
HBM = pl.BlockSpec(memory_space=pltpu.HBM)
MEGA = 1 << 20
REMOTE_LIMIT = 44
INNER_LIMIT = 39


def dot(a, b):
    return jnp.dot(a, b, preferred_element_type=F32)


def dot_nt(a, b):
    return lax.dot_general(a, b, (((1,), (1,)), ((), ())), preferred_element_type=F32)


def onehot(index, size):
    place = lax.broadcasted_iota(jnp.int32, (CHUNK, index.shape[1]), 0).astype(F32).astype(BF16)
    parts = []
    for start in range(0, size, CHUNK):
        at = jnp.broadcast_to((index - start).astype(F32).astype(BF16), place.shape)
        parts.append(jnp.where(place == at, jnp.ones_like(place), jnp.zeros_like(place)))
    return parts[0] if len(parts) == 1 else jnp.concatenate(parts, axis=0)


def start_all(pairs, sems):
    copies = [pltpu.make_async_copy(a, b, sems.at[i]) for i, (a, b) in enumerate(pairs)]
    for copy in copies:
        copy.start()
    return copies


def rms_scale(values, gain):
    mean_sq = jnp.mean(values * values, axis=-1, keepdims=True)
    return values * lax.rsqrt(mean_sq + 1e-05) * gain


def send_kernel(x_hbm, w_hbm, halo_hbm, table_hbm, out_hbm, x_ref, w_ref, halo_ref, table_ref, out_ref, in_sems, out_sems):
    rows, width = x_ref.shape
    parts = 4
    step = width // parts
    pairs = []
    for part in range(parts):
        cols = pl.ds(part * step, step)
        pairs.append((x_hbm.at[:, cols], x_ref.at[:, cols]))
        pairs.append((w_hbm.at[cols], w_ref.at[cols]))
    pairs.append((halo_hbm, halo_ref))
    copies = start_all(pairs, in_sems)
    proj = None
    for part in range(parts):
        copies[2 * part].wait()
        copies[2 * part + 1].wait()
        piece = dot(x_ref[:, part * step : (part + 1) * step], w_ref[part * step : (part + 1) * step])
        proj = piece if proj is None else proj + piece
    proj_t = jnp.transpose(proj).astype(BF16)
    for part in range(table_ref.shape[0]):
        table_ref[part] = proj_t[:, part * 128 : (part + 1) * 128]
    writes = [pltpu.make_async_copy(table_ref, table_hbm, out_sems.at[0])]
    writes[0].start()
    copies[2 * parts].wait()
    for pair in range(out_ref.shape[0] // 2):
        hot = jnp.concatenate(
            [onehot(halo_ref[pl.ds(2 * pair + k, 1), :], rows) for k in range(2)], axis=1
        )
        picked = dot(proj_t, hot).astype(BF16)
        out_ref[2 * pair] = picked[:, :128]
        out_ref[2 * pair + 1] = picked[:, 128:]
        two = pl.ds(2 * pair, 2)
        writes.append(pltpu.make_async_copy(out_ref.at[two], out_hbm.at[two], out_sems.at[1 + pair]))
        writes[-1].start()
    for write in writes:
        write.wait()


def edge_tiles(span, chunks, flat_ref, keys_ref, table_ref, recv_ref, bias_ref, pre_ref, hot_ref, agg_ref):
    rows = recv_ref.shape[1]
    begin, end = chunks

    def chunk_of(index, slot):
        at = 2 * (index - begin)
        chunk = jnp.concatenate([table_ref[at], table_ref[at + 1]], axis=1)
        return dot(chunk, onehot(slot - index * CHUNK, CHUNK))

    def indices(tile):
        key = keys_ref[tile]
        chunk = key >> 17
        slot = (chunk << 8) | (key & 255)
        recv = jnp.where((chunk >= begin) & (chunk < end), (key >> 8) & 511, -1)
        return recv, slot

    def gather(tile, place):
        recv, slot = indices(tile)
        low = jnp.maximum(flat_ref[tile * TILE] >> 17, begin)
        low = jnp.minimum(low, end - 2)
        hot = onehot(recv, rows)
        hot_ref[place] = hot
        pre_ref[place] = (
            dot(recv_ref[...], hot)
            + (chunk_of(low, slot) + chunk_of(low + 1, slot))
            + jnp.concatenate([bias_ref[...]] * (TILE // 128), axis=1)
        )

    def rest(tile, place):
        if end - begin > 2:
            slot = indices(tile)[1]
            low = jnp.minimum(jnp.maximum(flat_ref[tile * TILE] >> 17, begin), end - 2)
            high = jnp.minimum(flat_ref[tile * TILE + TILE - 1] >> 17, end - 1)

            def more(index, inner):
                pre_ref[place] += chunk_of(index, slot)
                return inner

            lax.fori_loop(low + 2, high + 1, more, 0)

    def scatter(place):
        half = 0.5 * pre_ref[place]
        message = (half + half * jnp.tanh(half)).astype(BF16)
        agg_ref[...] += dot_nt(hot_ref[place], message)

    start, stop = span

    @pl.when(start < stop)
    def _():
        gather(start, 0)
        rest(start, 0)

    def body(tile, carry):
        def step(now, later):
            scatter(now)
            gather(tile, later)
            rest(tile, later)

        odd = (tile - start) & 1
        pl.when(odd == 1)(lambda: step(0, 1))
        pl.when(odd == 0)(lambda: step(1, 0))
        return carry

    lax.fori_loop(start + 1, stop, body, 0)

    @pl.when(start < stop)
    def _():
        scatter((stop - 1 - start) & 1)


def tiles_of(flat_ref, tiles, bound):
    def count(tile, total):
        first = jnp.where((flat_ref[tile * TILE] >> 17) < bound, 1, 0)
        last = jnp.where((flat_ref[tile * TILE + TILE - 1] >> 17) < bound, 1, 0)
        return total[0] + first, total[1] + last

    return lax.fori_loop(0, tiles, count, (0, 0))


def local_kernel(
    flat_ref,
    keys_ref,
    bias_ref,
    x_hbm,
    w_hbm,
    table_hbm,
    w_message_hbm,
    w_lift_hbm,
    mats_hbm,
    agg_hbm,
    wide_hbm,
    x_ref,
    w_ref,
    table_ref,
    recv_ref,
    agg_ref,
    w_message_ref,
    w_lift_ref,
    pre_ref,
    hot_ref,
    bias_wide,
    sems,
):
    copies = start_all(
        [
            (x_hbm, x_ref),
            (w_hbm, w_ref),
            (table_hbm, table_ref),
            (w_message_hbm, w_message_ref),
            (w_lift_hbm, w_lift_ref),
        ],
        sems,
    )
    bias_wide[...] = jnp.transpose(jnp.broadcast_to(bias_ref[...], bias_wide.shape[::-1]))
    agg_ref[...] = jnp.zeros_like(agg_ref)
    copies[0].wait()
    copies[1].wait()
    proj = dot(x_ref[...], w_ref[...])
    recv_ref[...] = jnp.transpose(proj).astype(BF16)
    for copy in copies[2:]:
        copy.wait()
    early = start_all(
        [
            (recv_ref, mats_hbm.at[0]),
            (w_message_ref, mats_hbm.at[1]),
            (w_lift_ref, wide_hbm.at[0]),
            (x_ref, wide_hbm.at[1]),
        ],
        sems.at[pl.ds(6, 4)],
    )
    own = x_ref.shape[0] // CHUNK
    split = tiles_of(flat_ref, keys_ref.shape[0], own)[0]
    edge_tiles(
        (0, split), (0, own), flat_ref, keys_ref, table_ref, recv_ref, bias_wide, pre_ref, hot_ref, agg_ref
    )
    late = pltpu.make_async_copy(agg_ref, agg_hbm.at[0], sems.at[5])
    late.start()
    for copy in early:
        copy.wait()
    late.wait()


def finish_rows(agg, x, w_message, msg_gain, w_lift, attn_gain):
    high = agg.astype(BF16)
    low = (agg - high.astype(F32)).astype(BF16)
    mixed = dot(high, w_message) + dot(low, w_message)
    normed = rms_scale(mixed, msg_gain).astype(BF16)
    state = (x.astype(F32) + dot(normed, w_lift)).astype(BF16)
    return state, rms_scale(state.astype(F32), attn_gain).astype(BF16)


def remote_kernel(
    flat_ref,
    keys_ref,
    bias_ref,
    msg_gain_ref,
    attn_gain_ref,
    come_ref,
    mats_hbm,
    agg_hbm,
    wide_hbm,
    w_qkv_hbm,
    state_ref,
    attn_ref,
    top_ref,
    bottom_ref,
    w_q_ref,
    recv_ref,
    agg_in_ref,
    x_ref,
    w_message_ref,
    w_lift_ref,
    agg_ref,
    pre_ref,
    hot_ref,
    bias_wide,
    sems,
):
    rows = agg_ref.shape[0]
    first = pltpu.make_async_copy(mats_hbm.at[0], recv_ref, sems.at[0])
    first.start()
    agg_ref[...] = jnp.zeros_like(agg_ref)
    bias_wide[...] = jnp.transpose(jnp.broadcast_to(bias_ref[...], bias_wide.shape[::-1]))
    tiles = keys_ref.shape[0]
    own = rows // CHUNK
    split = tiles_of(flat_ref, tiles, own)[1]
    first.wait()
    later = start_all(
        [
            (agg_hbm.at[0], agg_in_ref),
            (mats_hbm.at[1], w_message_ref),
            (wide_hbm.at[0], w_lift_ref),
            (wide_hbm.at[1], x_ref),
            (w_qkv_hbm.at[:, pl.ds(0, w_q_ref.shape[1])], w_q_ref),
        ],
        sems.at[pl.ds(1, 5)],
    )
    edge_tiles(
        (split, tiles),
        (own, own + come_ref.shape[0] // 2),
        flat_ref,
        keys_ref,
        come_ref,
        recv_ref,
        bias_wide,
        pre_ref,
        hot_ref,
        agg_ref,
    )
    for copy in later:
        copy.wait()
    state, attn_in = finish_rows(
        agg_ref[...] + agg_in_ref[...],
        x_ref[...],
        w_message_ref[...],
        msg_gain_ref[...],
        w_lift_ref[...],
        attn_gain_ref[...],
    )
    state_ref[...] = state
    attn_ref[...] = attn_in
    top_ref[...] = attn_in[:WIN]
    bottom_ref[...] = attn_in[rows - WIN :]


def attend(q, k, v, apart, reach):
    lane = lax.broadcasted_iota(jnp.int32, q.shape, 1)
    zero = jnp.zeros_like(q)
    both = jnp.concatenate([jnp.where(lane < 64, q, zero), jnp.where(lane >= 64, q, zero)], axis=0)
    score = dot_nt(both, k)
    parts = []
    rows = q.shape[0]
    for head in range(2):
        one = score[head * rows : (head + 1) * rows]
        one = jnp.where(apart <= reach[head], one, NEG)
        top = jnp.max(one, axis=-1, keepdims=True)
        parts.append(jnp.exp2(one - top).astype(BF16))
    weights = jnp.concatenate(parts, axis=0)
    wide = jnp.concatenate([v, jnp.ones((v.shape[0], 128), BF16)], axis=1)
    mixed = dot(weights, wide)
    out = mixed[:, :128] / mixed[:, 128:]
    return jnp.where(lane < 64, out[:rows], out[rows:]).astype(BF16)


def distance(rows, keys):
    q_at = lax.broadcasted_iota(jnp.int32, (rows, keys), 0) + WIN
    k_at = lax.broadcasted_iota(jnp.int32, (rows, keys), 1)
    return jnp.abs(q_at - k_at), k_at


LOG2E = 1.4426950408889634


def project(rows, w_ref, scale=None):
    heads, size, width = w_ref.shape
    out = dot_nt(rows, w_ref[...].reshape(heads * size, width))
    return (out if scale is None else out * scale).astype(BF16)


def inner_kernel(
    reach_ref,
    state_ref,
    attn_ref,
    w_q_ref,
    w_qkv_hbm,
    w_out_hbm,
    q_ref,
    k_ref,
    v_ref,
    res_ref,
    w_k_ref,
    w_v_ref,
    w_out_ref,
    q_mid,
    mix_ref,
    apart_ref,
    sems,
):
    rows = attn_ref.shape[0]
    mid = rows - 2 * WIN
    size = w_k_ref.shape[1]
    copies = start_all(
        [
            (w_qkv_hbm.at[:, pl.ds(size, size)], w_k_ref),
            (w_qkv_hbm.at[:, pl.ds(2 * size, size)], w_v_ref),
            (w_out_hbm, w_out_ref),
        ],
        sems,
    )
    apart_ref[...] = distance(WIN, 3 * WIN)[0]
    q = project(attn_ref[...], w_q_ref, size**-0.5 * LOG2E)
    q_ref[pl.ds(0, WIN), :] = q[:WIN]
    q_ref[pl.ds(WIN, WIN), :] = q[rows - WIN :]
    q_mid[...] = q[WIN : rows - WIN]
    copies[0].wait()
    k_ref[...] = project(attn_ref[...], w_k_ref)
    copies[1].wait()
    v_ref[...] = project(attn_ref[...], w_v_ref)

    def body(pair, carry):
        lanes = pl.ds(pl.multiple_of(pair * 128, 128), 128)
        reach = (reach_ref[2 * pair], reach_ref[2 * pair + 1])
        for block in range(2):
            keys = pl.ds(block * WIN, 3 * WIN)
            mix_ref[pl.ds(block * WIN, WIN), lanes] = attend(
                q_mid[pl.ds(block * WIN, WIN), lanes],
                k_ref[keys, lanes],
                v_ref[keys, lanes],
                apart_ref[...],
                reach,
            )
        return carry

    lax.fori_loop(0, q_ref.shape[1] // 128, body, 0, unroll=8)
    copies[2].wait()
    res_ref[...] = (state_ref[pl.ds(WIN, mid), :].astype(F32) + dot(mix_ref[...], w_out_ref[...])).astype(BF16)


def outer_kernel(
    reach_ref,
    q_ref,
    left_ref,
    right_ref,
    k_ref,
    v_ref,
    state_ref,
    res_ref,
    w_k_ref,
    w_v_ref,
    w_out_ref,
    out_hbm,
    keys_ref,
    values_ref,
    apart_ref,
    mix_ref,
    fin_ref,
    sems,
):
    rows = k_ref.shape[0]
    early = pltpu.make_async_copy(res_ref, out_hbm.at[pl.ds(WIN, rows - 2 * WIN)], sems.at[0])
    early.start()
    me = lax.axis_index("node")
    last = lax.axis_size("node") - 1
    halo = jnp.concatenate([left_ref[...], right_ref[...]], axis=0)
    two = 2 * WIN
    keys_ref[0, pl.ds(WIN, two), :] = k_ref[pl.ds(0, two), :]
    keys_ref[1, pl.ds(0, two), :] = k_ref[pl.ds(rows - two, two), :]
    values_ref[0, pl.ds(WIN, two), :] = v_ref[pl.ds(0, two), :]
    values_ref[1, pl.ds(0, two), :] = v_ref[pl.ds(rows - two, two), :]
    apart, k_at = distance(WIN, 3 * WIN)
    apart_ref[0] = jnp.where((k_at < WIN) & (me == 0), BIG, apart)
    apart_ref[1] = jnp.where((k_at >= two) & (me == last), BIG, apart)
    k_halo = project(halo, w_k_ref)
    keys_ref[0, pl.ds(0, WIN), :] = k_halo[:WIN]
    keys_ref[1, pl.ds(two, WIN), :] = k_halo[WIN:]
    v_halo = project(halo, w_v_ref)
    values_ref[0, pl.ds(0, WIN), :] = v_halo[:WIN]
    values_ref[1, pl.ds(two, WIN), :] = v_halo[WIN:]

    def body(pair, carry):
        lanes = pl.ds(pl.multiple_of(pair * 128, 128), 128)
        reach = (reach_ref[2 * pair], reach_ref[2 * pair + 1])
        for block in range(2):
            mix_ref[pl.ds(block * WIN, WIN), lanes] = attend(
                q_ref[pl.ds(block * WIN, WIN), lanes],
                keys_ref[block, :, lanes],
                values_ref[block, :, lanes],
                apart_ref[block],
                reach,
            )
        return carry

    lax.fori_loop(0, q_ref.shape[1] // 128, body, 0, unroll=8)
    state = jnp.concatenate([state_ref[:WIN], state_ref[rows - WIN :]], axis=0)
    fin_ref[...] = (state.astype(F32) + dot(mix_ref[...], w_out_ref[...])).astype(BF16)
    ends = [
        pltpu.make_async_copy(fin_ref.at[pl.ds(0, WIN)], out_hbm.at[pl.ds(0, WIN)], sems.at[1]),
        pltpu.make_async_copy(
            fin_ref.at[pl.ds(WIN, WIN)], out_hbm.at[pl.ds(rows - WIN, WIN)], sems.at[2]
        ),
    ]
    for copy in ends:
        copy.start()
    early.wait()
    for copy in ends:
        copy.wait()


def call(kernel, name, out_shape, in_specs, out_specs, scratch, flops, moved, limit):
    return pl.pallas_call(
        kernel,
        name=name,
        out_shape=out_shape,
        in_specs=in_specs,
        out_specs=out_specs,
        scratch_shapes=scratch,
        compiler_params=pltpu.CompilerParams(vmem_limit_bytes=limit * MEGA),
        cost_estimate=pl.CostEstimate(flops=flops, bytes_accessed=moved, transcendentals=0),
    )


def local(
    node_state,
    edge_recv,
    edge_send,
    halo_rows,
    window_reach,
    w_recv,
    w_send,
    edge_bias,
    w_message,
    msg_gain,
    w_lift,
    attn_gain,
    w_qkv,
    w_out,
):
    shape = jax.ShapeDtypeStruct
    rows, width = node_state.shape
    hidden = w_recv.shape[1]
    peers, halo = halo_rows.shape[1:]
    edges = edge_recv.shape[0]
    tiles = edges // TILE
    dma = pltpu.SemaphoreType.DMA

    table, outgoing = call(
        send_kernel,
        "send",
        (shape((rows // 128, hidden, 128), BF16), shape((peers, hidden, halo), BF16)),
        [HBM] * 3,
        (HBM, HBM),
        [
            pltpu.VMEM((rows, width), BF16),
            pltpu.VMEM((width, hidden), BF16),
            pltpu.VMEM((peers, halo), jnp.int32),
            pltpu.VMEM((rows // 128, hidden, 128), BF16),
            pltpu.VMEM((peers, hidden, halo), BF16),
            dma((9,)),
            dma((1 + peers // 2,)),
        ],
        4 << 30,
        4 * MEGA,
        60,
    )(node_state, w_send, halo_rows.reshape(peers, halo))
    incoming = lax.all_to_all(outgoing, "node", split_axis=0, concat_axis=0, tiled=True)

    flat = lax.sort(((edge_send >> 8) << 17) | (edge_recv << 8) | (edge_send & 255))
    keys = flat.reshape(tiles, 1, TILE)
    bias = edge_bias.reshape(1, hidden)
    mats, agg, wide = call(
        local_kernel,
        "local_edges",
        (
            shape((16, hidden, rows), BF16),
            shape((8, rows, hidden), F32),
            shape((8, rows, width), BF16),
        ),
        [SMEM] + [VMEM] * 2 + [HBM] * 5,
        (HBM,) * 3,
        [
            pltpu.VMEM((rows, width), BF16),
            pltpu.VMEM((width, hidden), BF16),
            pltpu.VMEM((rows // 128, hidden, 128), BF16),
            pltpu.VMEM((hidden, rows), BF16),
            pltpu.VMEM((rows, hidden), F32),
            pltpu.VMEM((hidden, hidden), BF16),
            pltpu.VMEM((hidden, width), BF16),
            pltpu.VMEM((2, hidden, TILE), F32),
            pltpu.VMEM((2, rows, TILE), BF16),
            pltpu.VMEM((hidden, 128), F32),
            dma((10,)),
        ],
        10 << 30,
        4 * MEGA,
        60,
    )(flat, keys, bias, node_state, w_recv, table, w_message, w_lift)
    w_qkv_t = jnp.transpose(w_qkv, (1, 2, 0))

    gain_m = msg_gain.reshape(1, hidden)
    gain_a = attn_gain.reshape(1, width)
    heads = w_qkv.shape[1]
    part = (heads, width // heads, width)
    state, attn_in, top, bottom, w_q = call(
        remote_kernel,
        "remote_edges",
        (
            shape((rows, width), BF16),
            shape((rows, width), BF16),
            shape((WIN, width), BF16),
            shape((WIN, width), BF16),
            shape(part, BF16),
        ),
        [SMEM] + [VMEM] * 5 + [HBM] * 4,
        (VMEM,) * 5,
        [
            pltpu.VMEM((hidden, rows), BF16),
            pltpu.VMEM((rows, hidden), F32),
            pltpu.VMEM((rows, width), BF16),
            pltpu.VMEM((hidden, hidden), BF16),
            pltpu.VMEM((hidden, width), BF16),
            pltpu.VMEM((rows, hidden), F32),
            pltpu.VMEM((2, hidden, TILE), F32),
            pltpu.VMEM((2, rows, TILE), BF16),
            pltpu.VMEM((hidden, 128), F32),
            dma((6,)),
        ],
        10 << 30,
        4 * MEGA,
        REMOTE_LIMIT,
    )(flat, keys, bias, gain_m, gain_a, incoming, mats, agg, wide, w_qkv_t)

    nodes = lax.axis_size("node")
    left = lax.ppermute(bottom, "node", [(i, (i + 1) % nodes) for i in range(nodes)])
    right = lax.ppermute(top, "node", [(i, (i - 1) % nodes) for i in range(nodes)])

    q_tb, k, v, res_mid, *rest = call(
        inner_kernel,
        "inner",
        (
            shape((2 * WIN, width), BF16),
            shape((rows, width), BF16),
            shape((rows, width), BF16),
            shape((rows - 2 * WIN, width), BF16),
            shape(part, BF16),
            shape(part, BF16),
            shape(w_out.shape, BF16),
        ),
        [SMEM] + [VMEM] * 3 + [HBM] * 2,
        (VMEM,) * 7,
        [
            pltpu.VMEM((rows - 2 * WIN, width), BF16),
            pltpu.VMEM((rows - 2 * WIN, width), BF16),
            pltpu.VMEM((WIN, 3 * WIN), jnp.int32),
            dma((3,)),
        ],
        10 << 30,
        12 * MEGA,
        INNER_LIMIT,
    )(window_reach, state, attn_in, w_q, w_qkv_t, w_out)

    return call(
        outer_kernel,
        "outer",
        shape((rows, width), BF16),
        [SMEM] + [VMEM] * 10,
        HBM,
        [
            pltpu.VMEM((2, 3 * WIN, width), BF16),
            pltpu.VMEM((2, 3 * WIN, width), BF16),
            pltpu.VMEM((2, WIN, 3 * WIN), jnp.int32),
            pltpu.VMEM((2 * WIN, width), BF16),
            pltpu.VMEM((2 * WIN, width), BF16),
            dma((3,)),
        ],
        6 << 30,
        12 * MEGA,
        24,
    )(window_reach, q_tb, left, right, k, v, state, res_mid, *rest)


def solution(mesh):
    split = ("dp", "node")
    in_specs = (P(split, None), P(split), P(split), P(split, None, None)) + (P(),) * 10
    return jax.shard_map(
        local, mesh=mesh, in_specs=in_specs, out_specs=P(split, None), check_vma=False
    )
```

```python
import jax
import jax.numpy as jnp
from jax import lax
from jax.experimental import pallas as pl
from jax.experimental.pallas import tpu as pltpu
from jax.sharding import PartitionSpec as P

WIN = 128
TILE = 256
CHUNK = 256
BIG = 1 << 20
NEG = -1e30
F32 = jnp.float32
BF16 = jnp.bfloat16
VMEM = pl.BlockSpec(memory_space=pltpu.VMEM)
SMEM = pl.BlockSpec(memory_space=pltpu.SMEM)
HBM = pl.BlockSpec(memory_space=pltpu.HBM)
MEGA = 1 << 20
REMOTE_LIMIT = 44
INNER_LIMIT = 39


def dot(a, b):
    return jnp.dot(a, b, preferred_element_type=F32)


def dot_nt(a, b):
    return lax.dot_general(a, b, (((1,), (1,)), ((), ())), preferred_element_type=F32)


def onehot(index, size):
    place = lax.broadcasted_iota(jnp.int32, (CHUNK, index.shape[1]), 0).astype(F32).astype(BF16)
    parts = []
    for start in range(0, size, CHUNK):
        at = jnp.broadcast_to((index - start).astype(F32).astype(BF16), place.shape)
        parts.append(jnp.where(place == at, jnp.ones_like(place), jnp.zeros_like(place)))
    return parts[0] if len(parts) == 1 else jnp.concatenate(parts, axis=0)


def start_all(pairs, sems):
    copies = [pltpu.make_async_copy(a, b, sems.at[i]) for i, (a, b) in enumerate(pairs)]
    for copy in copies:
        copy.start()
    return copies


def rms_scale(values, gain):
    mean_sq = jnp.mean(values * values, axis=-1, keepdims=True)
    return values * lax.rsqrt(mean_sq + 1e-05) * gain


def send_kernel(x_hbm, w_hbm, halo_hbm, table_hbm, out_hbm, x_ref, w_ref, halo_ref, table_ref, out_ref, in_sems, out_sems):
    rows, width = x_ref.shape
    parts = 4
    step = width // parts
    pairs = []
    for part in range(parts):
        cols = pl.ds(part * step, step)
        pairs.append((x_hbm.at[:, cols], x_ref.at[:, cols]))
        pairs.append((w_hbm.at[cols], w_ref.at[cols]))
    pairs.append((halo_hbm, halo_ref))
    copies = start_all(pairs, in_sems)
    proj = None
    for part in range(parts):
        copies[2 * part].wait()
        copies[2 * part + 1].wait()
        piece = dot(x_ref[:, part * step : (part + 1) * step], w_ref[part * step : (part + 1) * step])
        proj = piece if proj is None else proj + piece
    proj_t = jnp.transpose(proj).astype(BF16)
    for part in range(table_ref.shape[0]):
        table_ref[part] = proj_t[:, part * 128 : (part + 1) * 128]
    writes = [pltpu.make_async_copy(table_ref, table_hbm, out_sems.at[0])]
    writes[0].start()
    copies[2 * parts].wait()
    for pair in range(out_ref.shape[0] // 2):
        hot = jnp.concatenate(
            [onehot(halo_ref[pl.ds(2 * pair + k, 1), :], rows) for k in range(2)], axis=1
        )
        picked = dot(proj_t, hot).astype(BF16)
        out_ref[2 * pair] = picked[:, :128]
        out_ref[2 * pair + 1] = picked[:, 128:]
        two = pl.ds(2 * pair, 2)
        writes.append(pltpu.make_async_copy(out_ref.at[two], out_hbm.at[two], out_sems.at[1 + pair]))
        writes[-1].start()
    for write in writes:
        write.wait()


def edge_tiles(span, chunks, flat_ref, keys_ref, table_ref, recv_ref, bias_ref, pre_ref, hot_ref, agg_ref):
    rows = recv_ref.shape[1]
    begin, end = chunks

    def chunk_of(index, slot):
        at = 2 * (index - begin)
        chunk = jnp.concatenate([table_ref[at], table_ref[at + 1]], axis=1)
        return dot(chunk, onehot(slot - index * CHUNK, CHUNK))

    def indices(tile):
        key = keys_ref[tile]
        chunk = key >> 17
        slot = (chunk << 8) | (key & 255)
        recv = jnp.where((chunk >= begin) & (chunk < end), (key >> 8) & 511, -1)
        return recv, slot

    def gather(tile, place):
        recv, slot = indices(tile)
        low = jnp.maximum(flat_ref[tile * TILE] >> 17, begin)
        low = jnp.minimum(low, end - 2)
        hot = onehot(recv, rows)
        hot_ref[place] = hot
        pre_ref[place] = (
            dot(recv_ref[...], hot)
            + (chunk_of(low, slot) + chunk_of(low + 1, slot))
            + jnp.concatenate([bias_ref[...]] * (TILE // 128), axis=1)
        )

    def rest(tile, place):
        if end - begin > 2:
            slot = indices(tile)[1]
            low = jnp.minimum(jnp.maximum(flat_ref[tile * TILE] >> 17, begin), end - 2)
            high = jnp.minimum(flat_ref[tile * TILE + TILE - 1] >> 17, end - 1)

            def more(index, inner):
                pre_ref[place] += chunk_of(index, slot)
                return inner

            lax.fori_loop(low + 2, high + 1, more, 0)

    def scatter(place):
        half = 0.5 * pre_ref[place]
        message = (half + half * jnp.tanh(half)).astype(BF16)
        agg_ref[...] += dot_nt(hot_ref[place], message)

    start, stop = span

    @pl.when(start < stop)
    def _():
        gather(start, 0)
        rest(start, 0)

    def body(tile, carry):
        def step(now, later):
            scatter(now)
            gather(tile, later)
            rest(tile, later)

        odd = (tile - start) & 1
        pl.when(odd == 1)(lambda: step(0, 1))
        pl.when(odd == 0)(lambda: step(1, 0))
        return carry

    lax.fori_loop(start + 1, stop, body, 0)

    @pl.when(start < stop)
    def _():
        scatter((stop - 1 - start) & 1)


def tiles_of(flat_ref, tiles, bound):
    def count(tile, total):
        first = jnp.where((flat_ref[tile * TILE] >> 17) < bound, 1, 0)
        last = jnp.where((flat_ref[tile * TILE + TILE - 1] >> 17) < bound, 1, 0)
        return total[0] + first, total[1] + last

    return lax.fori_loop(0, tiles, count, (0, 0))


def local_kernel(
    flat_ref,
    keys_ref,
    bias_ref,
    x_hbm,
    w_hbm,
    table_hbm,
    w_message_hbm,
    w_lift_hbm,
    mats_hbm,
    agg_hbm,
    wide_hbm,
    x_ref,
    w_ref,
    table_ref,
    recv_ref,
    agg_ref,
    w_message_ref,
    w_lift_ref,
    pre_ref,
    hot_ref,
    bias_wide,
    sems,
):
    copies = start_all(
        [
            (x_hbm, x_ref),
            (w_hbm, w_ref),
            (table_hbm, table_ref),
            (w_message_hbm, w_message_ref),
            (w_lift_hbm, w_lift_ref),
        ],
        sems,
    )
    bias_wide[...] = jnp.transpose(jnp.broadcast_to(bias_ref[...], bias_wide.shape[::-1]))
    agg_ref[...] = jnp.zeros_like(agg_ref)
    copies[0].wait()
    copies[1].wait()
    proj = dot(x_ref[...], w_ref[...])
    recv_ref[...] = jnp.transpose(proj).astype(BF16)
    for copy in copies[2:]:
        copy.wait()
    early = start_all(
        [
            (recv_ref, mats_hbm.at[0]),
            (w_message_ref, mats_hbm.at[1]),
            (w_lift_ref, wide_hbm.at[0]),
            (x_ref, wide_hbm.at[1]),
        ],
        sems.at[pl.ds(6, 4)],
    )
    own = x_ref.shape[0] // CHUNK
    split = tiles_of(flat_ref, keys_ref.shape[0], own)[0]
    edge_tiles(
        (0, split), (0, own), flat_ref, keys_ref, table_ref, recv_ref, bias_wide, pre_ref, hot_ref, agg_ref
    )
    late = pltpu.make_async_copy(agg_ref, agg_hbm.at[0], sems.at[5])
    late.start()
    for copy in early:
        copy.wait()
    late.wait()


def finish_rows(agg, x, w_message, msg_gain, w_lift, attn_gain):
    high = agg.astype(BF16)
    low = (agg - high.astype(F32)).astype(BF16)
    mixed = dot(high, w_message) + dot(low, w_message)
    normed = rms_scale(mixed, msg_gain).astype(BF16)
    state = (x.astype(F32) + dot(normed, w_lift)).astype(BF16)
    return state, rms_scale(state.astype(F32), attn_gain).astype(BF16)


def remote_kernel(
    flat_ref,
    keys_ref,
    bias_ref,
    msg_gain_ref,
    attn_gain_ref,
    come_ref,
    mats_hbm,
    agg_hbm,
    wide_hbm,
    w_qkv_hbm,
    state_ref,
    attn_ref,
    bottom_ref,
    top_ref,
    w_q_ref,
    recv_ref,
    agg_in_ref,
    x_ref,
    w_message_ref,
    w_lift_ref,
    agg_ref,
    pre_ref,
    hot_ref,
    bias_wide,
    sems,
):
    rows = agg_ref.shape[0]
    first = pltpu.make_async_copy(mats_hbm.at[0], recv_ref, sems.at[0])
    first.start()
    agg_ref[...] = jnp.zeros_like(agg_ref)
    bias_wide[...] = jnp.transpose(jnp.broadcast_to(bias_ref[...], bias_wide.shape[::-1]))
    tiles = keys_ref.shape[0]
    own = rows // CHUNK
    split = tiles_of(flat_ref, tiles, own)[1]
    first.wait()
    later = start_all(
        [
            (agg_hbm.at[0], agg_in_ref),
            (mats_hbm.at[1], w_message_ref),
            (wide_hbm.at[0], w_lift_ref),
            (wide_hbm.at[1], x_ref),
            (w_qkv_hbm.at[:, pl.ds(0, w_q_ref.shape[1])], w_q_ref),
        ],
        sems.at[pl.ds(1, 5)],
    )
    edge_tiles(
        (split, tiles),
        (own, own + come_ref.shape[0] // 2),
        flat_ref,
        keys_ref,
        come_ref,
        recv_ref,
        bias_wide,
        pre_ref,
        hot_ref,
        agg_ref,
    )
    for copy in later:
        copy.wait()
    state, attn_in = finish_rows(
        agg_ref[...] + agg_in_ref[...],
        x_ref[...],
        w_message_ref[...],
        msg_gain_ref[...],
        w_lift_ref[...],
        attn_gain_ref[...],
    )
    state_ref[...] = state
    attn_ref[...] = attn_in
    top_ref[...] = attn_in[:WIN]
    bottom_ref[...] = attn_in[rows - WIN :]


def attend(q, k, v, apart, reach):
    lane = lax.broadcasted_iota(jnp.int32, q.shape, 1)
    zero = jnp.zeros_like(q)
    both = jnp.concatenate([jnp.where(lane < 64, q, zero), jnp.where(lane >= 64, q, zero)], axis=0)
    score = dot_nt(both, k)
    parts = []
    rows = q.shape[0]
    for head in range(2):
        one = score[head * rows : (head + 1) * rows]
        one = jnp.where(apart <= reach[head], one, NEG)
        top = jnp.max(one, axis=-1, keepdims=True)
        parts.append(jnp.exp2(one - top).astype(BF16))
    weights = jnp.concatenate(parts, axis=0)
    wide = jnp.concatenate([v, jnp.ones((v.shape[0], 128), BF16)], axis=1)
    mixed = dot(weights, wide)
    mine = jnp.where(jnp.concatenate([lane, lane], axis=1) % 128 < 64, mixed[:rows], mixed[rows:])
    return (mine[:, :128] / mine[:, 128:]).astype(BF16)


def distance(rows, keys):
    q_at = lax.broadcasted_iota(jnp.int32, (rows, keys), 0) + WIN
    k_at = lax.broadcasted_iota(jnp.int32, (rows, keys), 1)
    return jnp.abs(q_at - k_at), k_at


LOG2E = 1.4426950408889634


def project(rows, w_ref, scale=None):
    heads, size, width = w_ref.shape
    out = dot_nt(rows, w_ref[...].reshape(heads * size, width))
    return (out if scale is None else out * scale).astype(BF16)


def inner_kernel(
    reach_ref,
    state_ref,
    attn_ref,
    w_q_ref,
    w_qkv_hbm,
    w_out_hbm,
    q_ref,
    k_ref,
    v_ref,
    res_ref,
    w_k_ref,
    w_v_ref,
    w_out_ref,
    q_mid,
    mix_ref,
    apart_ref,
    sems,
):
    rows = attn_ref.shape[0]
    mid = rows - 2 * WIN
    size = w_k_ref.shape[1]
    copies = start_all(
        [
            (w_qkv_hbm.at[:, pl.ds(size, size)], w_k_ref),
            (w_qkv_hbm.at[:, pl.ds(2 * size, size)], w_v_ref),
            (w_out_hbm, w_out_ref),
        ],
        sems,
    )
    apart_ref[...] = distance(WIN, 3 * WIN)[0]
    q = project(attn_ref[...], w_q_ref, size**-0.5 * LOG2E)
    q_ref[pl.ds(0, WIN), :] = q[:WIN]
    q_ref[pl.ds(WIN, WIN), :] = q[rows - WIN :]
    q_mid[...] = q[WIN : rows - WIN]
    copies[0].wait()
    k_ref[...] = project(attn_ref[...], w_k_ref)
    copies[1].wait()
    v_ref[...] = project(attn_ref[...], w_v_ref)

    def body(pair, carry):
        lanes = pl.ds(pl.multiple_of(pair * 128, 128), 128)
        reach = (reach_ref[2 * pair], reach_ref[2 * pair + 1])
        for block in range(2):
            keys = pl.ds(block * WIN, 3 * WIN)
            mix_ref[pl.ds(block * WIN, WIN), lanes] = attend(
                q_mid[pl.ds(block * WIN, WIN), lanes],
                k_ref[keys, lanes],
                v_ref[keys, lanes],
                apart_ref[...],
                reach,
            )
        return carry

    lax.fori_loop(0, q_ref.shape[1] // 128, body, 0, unroll=8)
    copies[2].wait()
    res_ref[...] = (state_ref[pl.ds(WIN, mid), :].astype(F32) + dot(mix_ref[...], w_out_ref[...])).astype(BF16)


def outer_kernel(
    reach_ref,
    q_ref,
    right_ref,
    left_ref,
    k_ref,
    v_ref,
    state_ref,
    res_ref,
    w_k_ref,
    w_v_ref,
    w_out_ref,
    out_hbm,
    keys_ref,
    values_ref,
    apart_ref,
    mix_ref,
    fin_ref,
    sems,
):
    rows = k_ref.shape[0]
    early = pltpu.make_async_copy(res_ref, out_hbm.at[pl.ds(WIN, rows - 2 * WIN)], sems.at[0])
    early.start()
    me = lax.axis_index("node")
    last = lax.axis_size("node") - 1
    halo = jnp.concatenate([left_ref[...], right_ref[...]], axis=0)
    two = 2 * WIN
    apart, k_at = distance(WIN, 3 * WIN)
    apart_ref[0] = jnp.where((k_at < WIN) & (me == 0), BIG, apart)
    apart_ref[1] = jnp.where((k_at >= two) & (me == last), BIG, apart)
    keys_ref[...] = project(halo, w_k_ref)
    values_ref[...] = project(halo, w_v_ref)

    def join(own_ref, halo_ref, block, lanes):
        if block == 0:
            parts = [halo_ref[pl.ds(0, WIN), lanes], own_ref[pl.ds(0, two), lanes]]
        else:
            parts = [own_ref[pl.ds(rows - two, two), lanes], halo_ref[pl.ds(WIN, WIN), lanes]]
        return jnp.concatenate(parts, axis=0)

    def body(pair, carry):
        lanes = pl.ds(pl.multiple_of(pair * 128, 128), 128)
        reach = (reach_ref[2 * pair], reach_ref[2 * pair + 1])
        for block in range(2):
            mix_ref[pl.ds(block * WIN, WIN), lanes] = attend(
                q_ref[pl.ds(block * WIN, WIN), lanes],
                join(k_ref, keys_ref, block, lanes),
                join(v_ref, values_ref, block, lanes),
                apart_ref[block],
                reach,
            )
        return carry

    lax.fori_loop(0, q_ref.shape[1] // 128, body, 0, unroll=8)
    state = jnp.concatenate([state_ref[:WIN], state_ref[rows - WIN :]], axis=0)
    fin_ref[...] = (state.astype(F32) + dot(mix_ref[...], w_out_ref[...])).astype(BF16)
    ends = [
        pltpu.make_async_copy(fin_ref.at[pl.ds(0, WIN)], out_hbm.at[pl.ds(0, WIN)], sems.at[1]),
        pltpu.make_async_copy(
            fin_ref.at[pl.ds(WIN, WIN)], out_hbm.at[pl.ds(rows - WIN, WIN)], sems.at[2]
        ),
    ]
    for copy in ends:
        copy.start()
    early.wait()
    for copy in ends:
        copy.wait()


def call(kernel, name, out_shape, in_specs, out_specs, scratch, flops, moved, limit):
    return pl.pallas_call(
        kernel,
        name=name,
        out_shape=out_shape,
        in_specs=in_specs,
        out_specs=out_specs,
        scratch_shapes=scratch,
        compiler_params=pltpu.CompilerParams(vmem_limit_bytes=limit * MEGA),
        cost_estimate=pl.CostEstimate(flops=flops, bytes_accessed=moved, transcendentals=0),
    )


def local(
    node_state,
    edge_recv,
    edge_send,
    halo_rows,
    window_reach,
    w_recv,
    w_send,
    edge_bias,
    w_message,
    msg_gain,
    w_lift,
    attn_gain,
    w_qkv,
    w_out,
):
    shape = jax.ShapeDtypeStruct
    rows, width = node_state.shape
    hidden = w_recv.shape[1]
    peers, halo = halo_rows.shape[1:]
    edges = edge_recv.shape[0]
    tiles = edges // TILE
    dma = pltpu.SemaphoreType.DMA

    table, outgoing = call(
        send_kernel,
        "send",
        (shape((rows // 128, hidden, 128), BF16), shape((peers, hidden, halo), BF16)),
        [HBM] * 3,
        (HBM, HBM),
        [
            pltpu.VMEM((rows, width), BF16),
            pltpu.VMEM((width, hidden), BF16),
            pltpu.VMEM((peers, halo), jnp.int32),
            pltpu.VMEM((rows // 128, hidden, 128), BF16),
            pltpu.VMEM((peers, hidden, halo), BF16),
            dma((9,)),
            dma((1 + peers // 2,)),
        ],
        4 << 30,
        4 * MEGA,
        60,
    )(node_state, w_send, halo_rows.reshape(peers, halo))
    incoming = lax.all_to_all(outgoing, "node", split_axis=0, concat_axis=0, tiled=True)

    flat = lax.sort(((edge_send >> 8) << 17) | (edge_recv << 8) | (edge_send & 255))
    keys = flat.reshape(tiles, 1, TILE)
    bias = edge_bias.reshape(1, hidden)
    mats, agg, wide = call(
        local_kernel,
        "local_edges",
        (
            shape((16, hidden, rows), BF16),
            shape((8, rows, hidden), F32),
            shape((8, rows, width), BF16),
        ),
        [SMEM] + [VMEM] * 2 + [HBM] * 5,
        (HBM,) * 3,
        [
            pltpu.VMEM((rows, width), BF16),
            pltpu.VMEM((width, hidden), BF16),
            pltpu.VMEM((rows // 128, hidden, 128), BF16),
            pltpu.VMEM((hidden, rows), BF16),
            pltpu.VMEM((rows, hidden), F32),
            pltpu.VMEM((hidden, hidden), BF16),
            pltpu.VMEM((hidden, width), BF16),
            pltpu.VMEM((2, hidden, TILE), F32),
            pltpu.VMEM((2, rows, TILE), BF16),
            pltpu.VMEM((hidden, 128), F32),
            dma((10,)),
        ],
        10 << 30,
        4 * MEGA,
        60,
    )(flat, keys, bias, node_state, w_recv, table, w_message, w_lift)
    w_qkv_t = jnp.transpose(w_qkv, (1, 2, 0))

    gain_m = msg_gain.reshape(1, hidden)
    gain_a = attn_gain.reshape(1, width)
    heads = w_qkv.shape[1]
    part = (heads, width // heads, width)
    state, attn_in, bottom, top, w_q = call(
        remote_kernel,
        "remote_edges",
        (
            shape((rows, width), BF16),
            shape((rows, width), BF16),
            shape((WIN, width), BF16),
            shape((WIN, width), BF16),
            shape(part, BF16),
        ),
        [SMEM] + [VMEM] * 5 + [HBM] * 4,
        (VMEM,) * 5,
        [
            pltpu.VMEM((hidden, rows), BF16),
            pltpu.VMEM((rows, hidden), F32),
            pltpu.VMEM((rows, width), BF16),
            pltpu.VMEM((hidden, hidden), BF16),
            pltpu.VMEM((hidden, width), BF16),
            pltpu.VMEM((rows, hidden), F32),
            pltpu.VMEM((2, hidden, TILE), F32),
            pltpu.VMEM((2, rows, TILE), BF16),
            pltpu.VMEM((hidden, 128), F32),
            dma((6,)),
        ],
        10 << 30,
        4 * MEGA,
        REMOTE_LIMIT,
    )(flat, keys, bias, gain_m, gain_a, incoming, mats, agg, wide, w_qkv_t)

    nodes = lax.axis_size("node")
    left = lax.ppermute(bottom, "node", [(i, (i + 1) % nodes) for i in range(nodes)])
    right = lax.ppermute(top, "node", [(i, (i - 1) % nodes) for i in range(nodes)])

    q_tb, k, v, res_mid, *rest = call(
        inner_kernel,
        "inner",
        (
            shape((2 * WIN, width), BF16),
            shape((rows, width), BF16),
            shape((rows, width), BF16),
            shape((rows - 2 * WIN, width), BF16),
            shape(part, BF16),
            shape(part, BF16),
            shape(w_out.shape, BF16),
        ),
        [SMEM] + [VMEM] * 3 + [HBM] * 2,
        (VMEM,) * 7,
        [
            pltpu.VMEM((rows - 2 * WIN, width), BF16),
            pltpu.VMEM((rows - 2 * WIN, width), BF16),
            pltpu.VMEM((WIN, 3 * WIN), jnp.int32),
            dma((3,)),
        ],
        10 << 30,
        12 * MEGA,
        INNER_LIMIT,
    )(window_reach, state, attn_in, w_q, w_qkv_t, w_out)

    return call(
        outer_kernel,
        "outer",
        shape((rows, width), BF16),
        [SMEM] + [VMEM] * 10,
        HBM,
        [
            pltpu.VMEM((2 * WIN, width), BF16),
            pltpu.VMEM((2 * WIN, width), BF16),
            pltpu.VMEM((2, WIN, 3 * WIN), jnp.int32),
            pltpu.VMEM((2 * WIN, width), BF16),
            pltpu.VMEM((2 * WIN, width), BF16),
            dma((3,)),
        ],
        6 << 30,
        12 * MEGA,
        24,
    )(window_reach, q_tb, right, left, k, v, state, res_mid, *rest)


def solution(mesh):
    split = ("dp", "node")
    in_specs = (P(split, None), P(split), P(split), P(split, None, None)) + (P(),) * 10
    return jax.shard_map(
        local, mesh=mesh, in_specs=in_specs, out_specs=P(split, None), check_vma=False
    )
```
